256 devices in a mesh: lat: 4 (over y_hi, core), lon: 64 (over x, y_lo, z).
Axes of the slice: x: 4, y: 4 (y_hi: 2, y_lo: 2; y = y_hi * 2 + y_lo), z: 8, core: 2. Of those that a mesh axis runs over, the one named last changes fastest.
Arguments:
- field: bfloat16 [64, 4096, 256], P('lat', 'lon'), may hold values from -6 to 6
- filters: bfloat16 [64, 4, 9, 264], P('lat'), may hold values from -0.1875 to 0.1875
- sector_width: int32 [8], P('lat'), may hold values from 1 to 2, as said below
- block_offset: int32 [8, 4], P('lat'), may hold values from -8 to 7, as said below
- mixing: bfloat16 [9, 32, 256], replicated, may hold values from -0.375 to 0.375
Outputs:
- output: bfloat16 [64, 4096, 256], P('lat', 'lon')
The draws below stay inside these ranges and needn't reach their ends.
Inputs may be any that keep to these rules, and one draw needn't show every extreme that they name: `sector_width`: the last row group has width 2, some row group has width 1. `block_offset`: in units of 8 longitudes; the last row group holds both ends of the range.
All inputs are finite; a program needn't handle non-finite values.
Results may differ from the reference program's by a relative error of at most 0.0049.
Values may be sent and summed in bfloat16 or wider, within the bound.
No kernel may reach another device: no remote copies, remote signals or barrier semaphores. Data moves between devices by JAX's collectives and lax.ppermute only.
A program may use at most 128 MiB of HBM per device.

```python
import jax
import jax.numpy as jnp
from jax import lax

K = 9
C = 256
G = 8
R = 16
RG = 8
NB = 4
BW = 8
SMAX = 2
LON_DEV = 64
CG = 32
RSPAN = 33
NROWS = 64
NLON = 4096


def draw_sector_width(key, part):
    key = jax.random.fold_in(key, 11)
    groups = NROWS // RG
    first_key = jax.random.fold_in(key, 1)
    second_key = jax.random.fold_in(key, 2)
    position = jnp.arange(groups, dtype=jnp.int32)
    values = jax.random.randint(first_key, (groups,), 1, SMAX + 1, dtype=jnp.int32)
    narrow = jax.random.randint(second_key, (), 0, groups - 1, dtype=jnp.int32)
    values = jnp.where(position == narrow, 1, values)
    values = jnp.where(position == groups - 1, SMAX, values)
    return values.astype(jnp.int32)


def draw_block_offset(key, part):
    key = jax.random.fold_in(key, 23)
    groups = NROWS // RG
    reach = LON_DEV // BW
    values = jax.random.randint(key, (groups, NB), -reach, reach, dtype=jnp.int32)
    values = values.at[groups - 1, 0].set(-reach)
    values = values.at[groups - 1, 1].set(reach - 1)
    return values.astype(jnp.int32)


def shard_levels(own_key, dims, cuts, least, high):
    factor_of = 1.0
    for dim, parts in cuts:
        draws = jax.random.uniform(jax.random.fold_in(jax.random.fold_in(own_key, 6), dim), (parts,), jnp.float32, least / len(cuts), high / len(cuts))
        factor_of = factor_of * jnp.repeat(jnp.exp(draws), dims[dim] // parts).reshape((-1,) + (1,) * (len(dims) - 1 - dim))
    return factor_of


def noise(key, shape, scale, most, split=(), held_as=jnp.bfloat16):
    factor_of = shard_levels(key, shape, split, -0.22, 0.18) if split else 1.0
    result = jax.random.normal(key, shape, jnp.float32) * scale * factor_of
    return jnp.minimum(jnp.maximum(result, -most), most).astype(held_as)


def setup_inputs(seed: int = 0) -> dict:
    key_of = jax.random.split(jax.random.key(seed), 6)
    return {
        "field": noise(key_of[0], (NROWS, NLON, C), 1.0, 6.0, ((0, 4), (1, 64))),
        "filters": noise(key_of[1], (NROWS, NB, K, RSPAN * BW), (RSPAN * NB * BW) ** -0.5, 0.1875, ((0, 4),)),
        "sector_width": draw_sector_width(jax.random.fold_in(key_of[5], 71), 0),
        "block_offset": draw_block_offset(jax.random.fold_in(key_of[5], 71), 0),
        "mixing": noise(key_of[4], (K, CG, C), (K * CG) ** -0.5, 0.375),
    }


def reference(field, filters, sector_width, block_offset, mixing):
    halo_lon = SMAX * LON_DEV
    padded = jnp.pad(field, ((R, R), (0, 0), (0, 0)))
    wrapped = jnp.concatenate([padded[:, NLON - halo_lon:], padded, padded[:, :halo_lon]], axis=1)
    shifts = (BW * block_offset * sector_width[:, None]).astype(jnp.int32)
    mix_table = mixing.astype(jnp.float32).reshape(K, CG, G, CG)

    def one_row(row_index):
        row_group = row_index // RG
        weights = filters[row_index].astype(jnp.float32).reshape(NB, K, 2 * R + 1, BW)
        response_sum = jnp.zeros((K, NLON, C), jnp.float32)
        for block_index in range(NB):
            start = (halo_lon + shifts[row_group, block_index]).astype(jnp.int32)
            window = lax.dynamic_slice(wrapped, (row_index.astype(jnp.int32), start, jnp.int32(0)), (2 * R + 1, NLON + BW - 1, C)).astype(jnp.float32)
            for column in range(BW):
                response_sum = response_sum + jnp.einsum('kr,rlc->klc', weights[block_index, :, :, column], window[:, column:column + NLON])
        rounded = lax.optimization_barrier(response_sum.astype(jnp.bfloat16))
        response = rounded.astype(jnp.float32).reshape(K, NLON, G, CG)
        mixed = jnp.einsum('klgc,kcgo->lgo', response, mix_table)
        return mixed.reshape(NLON, C).astype(jnp.bfloat16)

    return lax.map(one_row, jnp.arange(NROWS, dtype=jnp.int32))
```

```python
import functools

import jax
import jax.numpy as jnp
from jax import lax
from jax.experimental import pallas as pl
from jax.experimental.pallas import tpu as pltpu
from jax.sharding import PartitionSpec as P

K = 9
G = 8
R = 16
RG = 8
NB = 4
BW = 8
SMAX = 2
SPAN = 2 * R + 1
J = 2
T = BW + J - 1

SWAP = [(0, 1), (1, 0), (2, 3), (3, 2)]
ACROSS = [(0, 2), (2, 0), (1, 3), (3, 1)]


def from_behind(value, steps):
    count = lax.axis_size("lon")
    pairs = [(source, (source + steps) % count) for source in range(count)]
    return lax.ppermute(value, "lon", pairs)


def conv_kernel(depths, shift_ref, *refs):
    parts = len(depths)
    pieces = [refs[5 * i : 5 * i + 5] for i in range(parts)]
    refs = refs[5 * parts :]
    lhs_ref, mix_ref, out_ref = refs[:3]
    exts = refs[3 : 3 + parts]
    resp_ref, mixed_ref, sems = refs[3 + parts :]
    lon = pieces[0][0].shape[0]
    half = lon // 2
    steps = half // J
    copies = []
    for i in range(parts):
        for n in range(5):
            copy = pltpu.make_async_copy(
                pieces[i][n], exts[i].at[pl.ds(n * lon, lon)], sems.at[i, n]
            )
            copy.start()
            copies.append(copy)
    for copy in copies:
        copy.wait()

    def group(g, carry):
        def step(jb, carry):
            columns = []
            for side in range(2):
                rows = []
                for i in range(parts):
                    for b in range(NB):
                        start = SMAX * lon + shift_ref[g, b] + jb * J + side * half
                        window = exts[i][pl.ds(start, T)]
                        rows.append(window.reshape(T * depths[i], window.shape[2]))
                columns.append(jnp.concatenate(rows, axis=0))
            right = jnp.concatenate(columns, axis=1)
            resp = jnp.dot(lhs_ref[g], right, preferred_element_type=jnp.float32)
            resp = resp.astype(jnp.bfloat16)
            width = resp.shape[1]
            for k in range(K):
                resp_ref[pl.ds(pl.multiple_of(jb * 16, 16), 16), k * width : (k + 1) * width] = (
                    resp[k * 16 : (k + 1) * 16]
                )
            return carry

        lax.fori_loop(0, steps, step, 0, unroll=2)
        mixed = jnp.dot(resp_ref[...], mix_ref[...], preferred_element_type=jnp.float32)
        chans = mixed.shape[1] // 2
        for side in range(2):
            mixed_ref[side] = mixed[:, side * chans : (side + 1) * chans]
            for p in range(RG):
                rows = mixed_ref[side, pl.ds(p, half, stride=RG), :]
                out_ref[g, p, side * half : (side + 1) * half, :] = rows.astype(jnp.bfloat16)
        return carry

    lax.fori_loop(0, 2, group, 0)


def conv(shifts, pieces, lhs, mix):
    parts = len(pieces)
    lon, _, chans = pieces[0][0].shape
    depths = [p[0].shape[1] for p in pieces]
    vmem = pl.BlockSpec(memory_space=pltpu.VMEM)
    hbm = pl.BlockSpec(memory_space=pl.ANY)
    flat = [x for p in pieces for x in p]
    out = pl.pallas_call(
        functools.partial(conv_kernel, depths),
        out_shape=jax.ShapeDtypeStruct((2, RG, lon, chans), jnp.bfloat16),
        in_specs=[pl.BlockSpec(memory_space=pltpu.SMEM)] + [hbm] * len(flat) + [vmem, vmem],
        out_specs=vmem,
        scratch_shapes=[pltpu.VMEM((5 * lon, d, chans), jnp.bfloat16) for d in depths]
        + [
            pltpu.VMEM((lon // 2 * RG, K * 2 * chans), jnp.bfloat16),
            pltpu.VMEM((2, lon // 2 * RG, chans), jnp.float32),
            pltpu.SemaphoreType.DMA((parts, 5)),
        ],
        compiler_params=pltpu.CompilerParams(vmem_limit_bytes=48 << 20),
        cost_estimate=pl.CostEstimate(
            flops=2 * lhs.size * lon // J * chans, bytes_accessed=8 << 20, transcendentals=0
        ),
    )(shifts, *flat, lhs, mix)
    return out.reshape(2 * RG, lon, chans)


def left_sides(weights):
    rows = weights.shape[0]
    tall = rows + 2 * R
    at = lambda d: lax.broadcasted_iota(jnp.int32, (rows, SPAN, BW, J, T, tall), d)
    place = ((at(5) == at(0) + at(1)) & (at(4) == at(2) + at(3))).astype(jnp.bfloat16)
    place = place.reshape(rows, SPAN * BW, J * T * tall)
    flat = weights.reshape(rows, NB * K, SPAN * BW)
    spread = jnp.einsum("ixr,irc->ixc", flat, place, preferred_element_type=jnp.float32)
    spread = spread.astype(jnp.bfloat16).reshape(2, RG, NB, K, J, T, tall)
    return spread.transpose(0, 3, 4, 1, 2, 5, 6).reshape(2, K * J * RG, NB, T, tall)


def on_device(field, filters, sector_width, block_offset, mixing):
    rows, lon, chans = field.shape
    half = chans // 2
    lat = lax.axis_index("lat")
    upper, core = lat // 2, lat % 2

    turned = field.transpose(1, 0, 2)
    low, high = turned[:, :, :half], turned[:, :, half:]
    first = core == 0
    mine = jnp.where(first, low, high)
    got = lax.ppermute(jnp.where(first, high, low), "lat", SWAP)
    top, bottom = jnp.where(first, mine, got), jnp.where(first, got, mine)
    own = jnp.concatenate([top, bottom], axis=1)
    edge = lax.ppermute(jnp.where(upper == 0, bottom, top), "lat", ACROSS)

    def sectors(x):
        west, east = from_behind(x, 1), from_behind(x, -1)
        return [from_behind(west, 1), west, x, east, from_behind(east, -1)]

    own_sectors = sectors(own)
    edge_sectors = sectors(edge)

    shifts = BW * block_offset * sector_width[:, None]
    other_shifts = lax.ppermute(shifts, "lat", SWAP)
    other_filters = lax.ppermute(filters, "lat", SWAP)
    far = core == upper
    far_shifts = jnp.where(far, shifts, other_shifts)
    near_shifts = jnp.where(far, other_shifts, shifts)
    far_left = left_sides(jnp.where(far, filters, other_filters))
    near_left = left_sides(jnp.where(far, other_filters, filters))

    def columns(left, start, width):
        left = lax.dynamic_slice_in_dim(left, start, width, axis=4)
        return left.reshape(2, K * J * RG, NB * T * width)

    far_lhs = columns(far_left, R * (1 - upper), 2 * R)
    near_lhs = jnp.concatenate(
        [columns(near_left, R * upper, 2 * R), columns(near_left, 2 * R * (1 - upper), R)], axis=2
    )

    group_chans = chans // G
    side = lax.dynamic_slice_in_dim(mixing, core * half, half, axis=2)
    tiled = jnp.tile(side, (1, chans // group_chans, 2))
    row_at = lax.broadcasted_iota(jnp.int32, (chans, chans), 0) // group_chans
    col_at = lax.broadcasted_iota(jnp.int32, (chans, chans), 1) // group_chans
    mix = jnp.where((row_at == col_at)[None], tiled, jnp.zeros_like(tiled))
    mix = mix.reshape(K * chans, chans)

    far_out = conv(far_shifts, [own_sectors], far_lhs, mix)
    near_out = conv(near_shifts, [own_sectors, edge_sectors], near_lhs, mix)

    kept = jnp.where(far, far_out, near_out)
    other = lax.ppermute(jnp.where(far, near_out, far_out), "lat", SWAP)
    return jnp.concatenate([jnp.where(first, kept, other), jnp.where(first, other, kept)], axis=2)


def solution(mesh):
    return jax.shard_map(
        on_device,
        mesh=mesh,
        in_specs=(P("lat", "lon", None), P("lat", None, None, None), P("lat"), P("lat", None), P()),
        out_specs=P("lat", "lon", None),
        check_vma=False,
    )
```

```python
import functools

import jax
import jax.numpy as jnp
from jax import lax
from jax.experimental import pallas as pl
from jax.experimental.pallas import tpu as pltpu
from jax.sharding import PartitionSpec as P

K = 9
G = 8
R = 16
RG = 8
NB = 4
BW = 8
SMAX = 2
J = 2
T = BW + J - 1
SECTORS = 2 * SMAX + 1
PADDED = 384
VMEM = pl.BlockSpec(memory_space=pltpu.VMEM)
SMEM = pl.BlockSpec(memory_space=pltpu.SMEM)
ANY = pl.BlockSpec(memory_space=pl.ANY)


def send(value, across, core, steps):
    count = lax.axis_size("lon")
    pairs = []
    for lat in range(4):
        target = (lat ^ (2 * across)) ^ core
        for lon in range(count):
            pairs.append((lat * count + lon, target * count + (lon + steps) % count))
    return lax.ppermute(value, ("lat", "lon"), pairs)


def prep_kernel(place_ref, filt_ref, far_ref, near_ref, edge_ref, spread_ref, pick_ref, pick_edge_ref):
    upper = place_ref[0]
    far = place_ref[1]
    deep = NB * PADDED
    wide = BW * NB * 2 * R

    def fill(ref, target):
        width = ref.shape[1]

        def some(n, carry):
            row = n * 128 + lax.broadcasted_iota(jnp.int32, (128, width), 0)
            hit = jnp.where(row == target, 1.0, 0.0)
            ref[pl.ds(pl.multiple_of(n * 128, 128), 128), :] = hit.astype(jnp.bfloat16)
            return carry

        lax.fori_loop(0, deep // 128, some, 0)

    def own_target(start):
        c = lax.broadcasted_iota(jnp.int32, (1, wide), 1)
        return ((c >> 5) & 3) * PADDED + ((c & 31) + start) * BW + (c >> 7)

    def edge_target(start, j):
        c = lax.broadcasted_iota(jnp.int32, (1, T * NB * R), 1)
        t = (c >> 6) - j
        at = ((c >> 4) & 3) * PADDED + ((c & 15) + start) * BW + t
        return jnp.where((t >= 0) & (t < BW), at, -1)

    for j in range(J):
        fill(pick_edge_ref.at[j], edge_target(2 * R * (1 - upper), j))
    for which in range(2):
        half = jnp.where(far == 1, which, 1 - which)
        out_ref = (far_ref, near_ref)[which]
        fill(pick_ref, own_target(R * (1 - upper) if which == 0 else R * upper))
        for g in range(2):
            for p in range(RG):
                i = g * RG + p
                for b in range(NB):
                    x = filt_ref[half, i, b].astype(jnp.float32)
                    if i:
                        x = pltpu.roll(x, BW * i, 1)
                    for n in range(PADDED // 128):
                        at = b * PADDED // 128 + n
                        spread_ref[at, pl.ds(p, K, stride=RG), :] = x[:, n * 128 : (n + 1) * 128]
            spread = jnp.concatenate([spread_ref[n] for n in range(deep // 128)], axis=1)
            spread = spread.astype(jnp.bfloat16)
            own = jnp.dot(spread, pick_ref[...], preferred_element_type=jnp.float32)
            blank = jnp.zeros((RG, 128), jnp.float32)
            for k in range(K):
                rows = own[k * RG : (k + 1) * RG]
                first = jnp.concatenate([rows, blank], axis=1)
                second = jnp.concatenate([blank, rows], axis=1)
                both = jnp.concatenate([first, second], axis=0)
                out_ref[g, k * 16 : (k + 1) * 16, :] = both.astype(jnp.bfloat16)
            if which:
                edges = [
                    jnp.dot(spread, pick_edge_ref[j], preferred_element_type=jnp.float32)
                    for j in range(J)
                ]
                for k in range(K):
                    both = jnp.concatenate([e[k * RG : (k + 1) * RG] for e in edges], axis=0)
                    edge_ref[g, k * 16 : (k + 1) * 16, :] = both.astype(jnp.bfloat16)


def left_sides(place, filters):
    wide, edge, deep = T * NB * 2 * R, T * NB * R, NB * PADDED
    return pl.pallas_call(
        prep_kernel,
        out_shape=[
            jax.ShapeDtypeStruct((2, K * J * RG, width), jnp.bfloat16)
            for width in (wide, wide, edge)
        ],
        in_specs=[SMEM, VMEM],
        out_specs=[VMEM] * 3,
        scratch_shapes=[
            pltpu.VMEM((deep // 128, K * RG, 128), jnp.float32),
            pltpu.VMEM((deep, BW * NB * 2 * R), jnp.bfloat16),
            pltpu.VMEM((J, deep, edge), jnp.bfloat16),
        ],
        compiler_params=pltpu.CompilerParams(vmem_limit_bytes=24 << 20),
        cost_estimate=pl.CostEstimate(flops=8 * 10**9, bytes_accessed=4 << 20, transcendentals=0),
    )(place, filters)


def fetch(place_ref, pieces, ext_ref, sems):
    lon = pieces[0].shape[0]
    copies = []
    for n, piece in enumerate(pieces):
        row_set, sector = n // SECTORS, n % SECTORS
        target = ext_ref.at[pl.ds(sector * lon, lon)]
        if len(pieces) > SECTORS:
            core = place_ref[2]
            first = jnp.where(core == row_set, 0, R)
            target = ext_ref.at[pl.ds(sector * lon, lon), pl.ds(pl.multiple_of(first, R), R)]
        copies.append(pltpu.make_async_copy(piece, target, sems.at[n]))
    for copy in copies:
        copy.start()
    for copy in copies:
        copy.wait()


def product(left, ext_ref, shift_ref, g, jb, lon):
    columns = []
    for side in range(2):
        at = SMAX * lon + jb * J + side * (lon // 2)
        starts = [at + shift_ref[g, b] for b in range(NB)]
        rows = [ext_ref[starts[b] + t] for t in range(T) for b in range(NB)]
        columns.append(jnp.concatenate(rows, axis=0))
    right = jnp.concatenate(columns, axis=1)
    return jnp.dot(left, right, preferred_element_type=jnp.float32)


def keep(resp_ref, resp, jb):
    resp = resp.astype(jnp.bfloat16)
    width = resp.shape[1]
    rows = pl.ds(pl.multiple_of(jb * 16, 16), 16)
    for k in range(K):
        resp_ref[rows, k * width : (k + 1) * width] = resp[k * 16 : (k + 1) * 16]


def mix_rows(resp_ref, mix_ref, mixed_ref, out_ref, g):
    mixed = jnp.dot(resp_ref[...], mix_ref[...], preferred_element_type=jnp.float32)
    chans = mixed.shape[1] // 2
    half = mixed.shape[0] // RG
    for side in range(2):
        mixed_ref[side] = mixed[:, side * chans : (side + 1) * chans]
        for p in range(RG):
            rows = mixed_ref[side, pl.ds(p, half, stride=RG), :]
            out_ref[g, p, side * half : (side + 1) * half, :] = rows.astype(jnp.bfloat16)


def over_groups(steps, step, after):
    def group(g, carry):
        def one(jb, carry):
            step(g, jb)
            return carry

        lax.fori_loop(0, steps, one, 0, unroll=True)
        after(g)
        return carry

    lax.fori_loop(0, 2, group, 0)


def far_kernel(place_ref, shift_ref, *refs):
    pieces = refs[: 2 * SECTORS]
    left_ref, mix_ref, out_ref, ext_ref, resp_ref, mixed_ref, sems = refs[2 * SECTORS :]
    lon = pieces[0].shape[0]
    fetch(place_ref, pieces, ext_ref, sems)
    over_groups(
        lon // 2 // J,
        lambda g, jb: keep(resp_ref, product(left_ref[g], ext_ref, shift_ref, g, jb, lon), jb),
        lambda g: mix_rows(resp_ref, mix_ref, mixed_ref, out_ref, g),
    )


def near_kernel(place_ref, shift_ref, *refs):
    pieces = refs[: 2 * SECTORS]
    left_ref, sums_ref, ext_ref, sems = refs[2 * SECTORS :]
    lon = pieces[0].shape[0]
    fetch(place_ref, pieces, ext_ref, sems)

    def step(g, jb):
        sums_ref[g, jb] = product(left_ref[g], ext_ref, shift_ref, g, jb, lon)

    over_groups(lon // 2 // J, step, lambda g: None)


def edge_kernel(place_ref, shift_ref, *refs):
    pieces = refs[:SECTORS]
    left_ref, mix_ref, sums_ref, out_ref, ext_ref, resp_ref, mixed_ref, sems = refs[SECTORS:]
    lon = pieces[0].shape[0]
    fetch(place_ref, pieces, ext_ref, sems)

    def step(g, jb):
        resp = sums_ref[g, jb] + product(left_ref[g], ext_ref, shift_ref, g, jb, lon)
        keep(resp_ref, resp, jb)

    over_groups(
        lon // 2 // J, step, lambda g: mix_rows(resp_ref, mix_ref, mixed_ref, out_ref, g)
    )


def conv(kernel, place, shifts, pieces, left, mix=None, sums=None):
    lon, _, chans = pieces[0].shape
    depth = R * (len(pieces) // SECTORS)
    half = lon // 2
    ext = [pltpu.VMEM((SECTORS * lon, depth, chans), jnp.bfloat16)]
    sems = [pltpu.SemaphoreType.DMA((len(pieces),))]
    if mix is None:
        out = jax.ShapeDtypeStruct((2, half // J, K * J * RG, 2 * chans), jnp.float32)
        scratch = ext + sems
    else:
        out = jax.ShapeDtypeStruct((2, RG, lon, chans), jnp.bfloat16)
        scratch = ext + [
            pltpu.VMEM((half * RG, K * 2 * chans), jnp.bfloat16),
            pltpu.VMEM((2, half * RG, chans), jnp.float32),
        ]
        scratch += sems
    arrays = [left] + [x for x in (mix, sums) if x is not None]
    return pl.pallas_call(
        kernel,
        out_shape=out,
        in_specs=[SMEM, SMEM] + [ANY] * len(pieces) + [VMEM] * len(arrays),
        out_specs=VMEM,
        scratch_shapes=scratch,
        compiler_params=pltpu.CompilerParams(vmem_limit_bytes=24 << 20),
        cost_estimate=pl.CostEstimate(
            flops=4 * left.size * half // J * 2 * chans, bytes_accessed=8 << 20, transcendentals=0
        ),
    )(place, shifts, *pieces, *arrays)


def after(value, *others):
    return lax.optimization_barrier((value, *others))[0]


def on_device(field, filters, sector_width, block_offset, mixing):
    rows, lon, chans = field.shape
    half = chans // 2
    lat = lax.axis_index("lat")
    upper, core = lat // 2, lat % 2
    first = core == 0
    far = core == upper
    place = jnp.stack([upper, far.astype(jnp.int32), core]).astype(jnp.int32)

    turned = field.transpose(1, 0, 2)
    low, high = turned[:, :, :half], turned[:, :, half:]
    mine, theirs = lax.optimization_barrier(
        (jnp.where(first, low, high), jnp.where(first, high, low))
    )
    got = send(theirs, 0, 1, 0)
    mine_w, mine_e = send(mine, 0, 0, 1), send(mine, 0, 0, -1)
    got_w, got_e = send(theirs, 0, 1, 1), send(theirs, 0, 1, -1)

    shifts = BW * block_offset * sector_width[:, None]
    filters = after(filters, mine)
    other_shifts = send(after(shifts, mine), 0, 1, 0)
    other_filters = send(filters, 0, 1, 0)
    far_shifts = jnp.where(far, shifts, other_shifts)
    near_shifts = jnp.where(far, other_shifts, shifts)
    both = jnp.stack([filters, other_filters])
    both = jnp.pad(both, ((0, 0),) * 4 + ((0, PADDED - both.shape[-1]),))
    far_left, near_left, edge_left = left_sides(place, both)

    group_chans = chans // G
    side = lax.dynamic_slice_in_dim(after(mixing, mine), core * half, half, axis=2)
    tiled = jnp.tile(side, (1, chans // group_chans, 2))
    row_at = lax.broadcasted_iota(jnp.int32, (chans, chans), 0) // group_chans
    col_at = lax.broadcasted_iota(jnp.int32, (chans, chans), 1) // group_chans
    mix = jnp.where((row_at == col_at)[None], tiled, jnp.zeros_like(tiled))
    mix = mix.reshape(K * chans, chans)

    edge = send(jnp.where(far, got, mine), 1, 0, 0)

    mine_w2, mine_e2 = send(mine_w, 0, 0, 1), send(mine_e, 0, 0, -1)
    got_w2, got_e2 = send(got_w, 0, 0, 1), send(got_e, 0, 0, -1)
    pieces = [mine_w2, mine_w, mine, mine_e, mine_e2, got_w2, got_w, got, got_e, got_e2]
    pieces = list(lax.optimization_barrier(tuple(pieces)))
    edge = after(edge, *pieces)
    edge_w, edge_e = send(edge, 0, 0, 1), send(edge, 0, 0, -1)
    sums = conv(near_kernel, place, near_shifts, pieces, near_left)
    edge_w, edge_e, sums = lax.optimization_barrier((edge_w, edge_e, sums))
    edge_w2, edge_e2 = send(edge_w, 0, 0, 1), send(edge_e, 0, 0, -1)
    pieces = list(lax.optimization_barrier((*pieces, sums))[:-1])
    far_out = conv(far_kernel, place, far_shifts, pieces, far_left, mix)
    edges = [edge_w2, edge_w, edge, edge_e, edge_e2]
    edges, far_out = lax.optimization_barrier((edges, far_out))
    near_out = conv(edge_kernel, place, near_shifts, edges, edge_left, mix, sums)

    far_out, near_out = (x.reshape(rows, lon, half) for x in (far_out, near_out))
    kept = jnp.where(far, far_out, near_out)
    other = send(jnp.where(far, near_out, far_out), 0, 1, 0)
    return jnp.concatenate([jnp.where(first, kept, other), jnp.where(first, other, kept)], axis=2)


def solution(mesh):
    return jax.shard_map(
        on_device,
        mesh=mesh,
        in_specs=(P("lat", "lon", None), P("lat", None, None, None), P("lat"), P("lat", None), P()),
        out_specs=P("lat", "lon", None),
        check_vma=False,
    )
```

```python
import functools

import jax
import jax.numpy as jnp
from jax import lax
from jax.experimental import pallas as pl
from jax.experimental.pallas import tpu as pltpu
from jax.sharding import PartitionSpec as P

K = 9
G = 8
R = 16
RG = 8
NB = 4
BW = 8
SMAX = 2
J = 2
T = BW + J - 1
SECTORS = 2 * SMAX + 1
PADDED = 384
VMEM = pl.BlockSpec(memory_space=pltpu.VMEM)
SMEM = pl.BlockSpec(memory_space=pltpu.SMEM)
ANY = pl.BlockSpec(memory_space=pl.ANY)


def lat_swap(value, flip):
    return lax.ppermute(value, "lat", [(lat, lat ^ flip) for lat in range(4)])


def pair_swap(value, odd):
    count = lax.axis_size("lon")
    pairs = [(s, (((s + odd) ^ 1) - odd) % count) for s in range(count)]
    return lax.ppermute(value, "lon", pairs)


def halo(value):
    near, back = pair_swap(value, 0), pair_swap(value, 1)
    return near, back


def beyond(near, back):
    return pair_swap(back, 0), pair_swap(near, 1)


def prep_kernel(place_ref, filt_ref, far_ref, near_ref, spread_ref, pick_ref):
    upper = place_ref[0]
    far = place_ref[1]
    deep, wide = NB * 128, T * NB * R

    row = lax.broadcasted_iota(jnp.int32, (deep, wide), 0)
    col = lax.broadcasted_iota(jnp.int32, (1, wide), 1)
    for j in range(J):
        t = (col >> 6) - j
        target = ((col >> 4) & 3) * 128 + (col & 15) * BW + t
        hit = jnp.where((row == target) & (t >= 0) & (t < BW), 1.0, 0.0)
        pick_ref[j] = hit.astype(jnp.bfloat16)

    for which in range(2):
        half = jnp.where(far == 1, which, 1 - which)
        base = 1 - upper if which == 0 else upper
        for g in range(2):
            for p in range(RG):
                i = g * RG + p
                for b in range(NB):
                    x = filt_ref[half, i, b].astype(jnp.float32)
                    if i:
                        x = pltpu.roll(x, BW * i, 1)
                    for n in range(PADDED // 128):
                        spread_ref[n, b, pl.ds(p, K, stride=RG), :] = x[:, n * 128 : (n + 1) * 128]

            def lay(band, n):
                left = jnp.concatenate([spread_ref[band, b] for b in range(NB)], axis=1)
                left = left.astype(jnp.bfloat16)
                sides = [
                    jnp.dot(left, pick_ref[j], preferred_element_type=jnp.float32)
                    for j in range(J)
                ]
                for k in range(K):
                    both = jnp.concatenate([s[k * RG : (k + 1) * RG] for s in sides], axis=0)
                    columns = slice(n * wide, (n + 1) * wide)
                    ref = (far_ref, near_ref)[which]
                    ref[g, k * 16 : (k + 1) * 16, columns] = both.astype(jnp.bfloat16)

            lay(base, 0)
            lay(base + 1, 1)
            if which:
                lay(2 * (1 - upper), 2)


def left_sides(place, filters):
    wide = T * NB * R
    return pl.pallas_call(
        prep_kernel,
        out_shape=[
            jax.ShapeDtypeStruct((2, K * J * RG, sets * wide), jnp.bfloat16) for sets in (2, 3)
        ],
        in_specs=[SMEM, VMEM],
        out_specs=[VMEM] * 2,
        scratch_shapes=[
            pltpu.VMEM((PADDED // 128, NB, K * RG, 128), jnp.float32),
            pltpu.VMEM((J, NB * 128, wide), jnp.bfloat16),
        ],
        compiler_params=pltpu.CompilerParams(vmem_limit_bytes=16 << 20),
        cost_estimate=pl.CostEstimate(flops=1, bytes_accessed=1, transcendentals=0),
    )(place, filters)


def fetch(place_ref, pieces, ext, sems):
    lon = pieces[0].shape[0]
    odd = place_ref[2]
    sectors = (SMAX, 3 - 2 * odd, 1 + 2 * odd, 4 - 4 * odd, 4 * odd)
    copies = []
    for n, piece in enumerate(pieces):
        target = ext.at[pl.ds(sectors[n] * lon, lon)]
        copies.append(pltpu.make_async_copy(piece, target, sems.at[n]))
    return copies


def product(left, exts, shifts, jb, lon):
    columns = []
    for side in range(2):
        at = SMAX * lon + jb * J + side * (lon // 2)
        starts = [at + shift for shift in shifts]
        rows = []
        for ext in exts:
            for first in range(0, ext.shape[1], R):
                for t in range(T):
                    for start in starts:
                        rows.append(ext[start + t, first : first + R, :])
        columns.append(jnp.concatenate(rows, axis=0))
    right = jnp.concatenate(columns, axis=1)
    return jnp.dot(left, right, preferred_element_type=jnp.float32)


def keep(resp_ref, resp, jb):
    resp = resp.astype(jnp.bfloat16)
    width = resp.shape[1]
    rows = pl.ds(pl.multiple_of(jb * 16, 16), 16)
    for k in range(K):
        resp_ref[rows, k * width : (k + 1) * width] = resp[k * 16 : (k + 1) * 16]


def mix_rows(resp_ref, mix_ref, mixed_ref, out_ref, g):
    mixed = jnp.dot(resp_ref[...], mix_ref[...], preferred_element_type=jnp.float32)
    chans = mixed.shape[1] // 2
    half = mixed.shape[0] // RG
    for side in range(2):
        mixed_ref[side] = mixed[:, side * chans : (side + 1) * chans]
        for p in range(RG):
            rows = mixed_ref[side, pl.ds(p, half, stride=RG), :]
            out_ref[g, p, side * half : (side + 1) * half, :] = rows.astype(jnp.bfloat16)


def conv_kernel(early, whiches, counts, place_ref, shift_ref, *refs):
    sets = []
    for count in counts:
        sets.append(refs[:count])
        refs = refs[count:]
    some = len(whiches)
    left_refs, mix_ref, refs = refs[:some], refs[some], refs[some + 1 :]
    if not early:
        done_refs, refs = refs[:some], refs[some:]
    out_refs, refs = refs[:some], refs[some:]
    exts, (resp_ref, mixed_ref, sems) = refs[: len(sets)], refs[len(sets) :]
    lon = sets[0][0].shape[0]
    copies = []
    for i, pieces in enumerate(sets):
        copies += fetch(place_ref, pieces, exts[i], sems.at[i])
    for copy in copies:
        copy.start()
    for copy in copies:
        copy.wait()
    for n, which in enumerate(whiches):
        left_ref, out_ref = left_refs[n], out_refs[n]

        def group(g, carry):
            shifts = [shift_ref[2 * which + g, b] for b in range(NB)]
            local = True
            for shift in shifts:
                local = local & (shift >= -lon) & (shift <= lon - BW)

            @pl.when(local if early else jnp.logical_not(local))
            def _():
                def step(jb, carry):
                    keep(resp_ref, product(left_ref[g], exts[: 1 + which], shifts, jb, lon), jb)
                    return carry

                lax.fori_loop(0, lon // 2 // J, step, 0, unroll=True)
                mix_rows(resp_ref, mix_ref, mixed_ref, out_ref, g)

            if not early:

                @pl.when(local)
                def _():
                    out_ref[g] = done_refs[n][g]

            return carry

        lax.fori_loop(0, 2, group, 0)


def conv(whiches, place, shifts, sets, lefts, mix, done=()):
    lon, _, chans = sets[0][0].shape
    half = lon // 2
    counts = [len(pieces) for pieces in sets]
    arrays = [*lefts, mix, *done]
    return pl.pallas_call(
        functools.partial(conv_kernel, not done, whiches, counts),
        out_shape=[jax.ShapeDtypeStruct((2, RG, lon, chans), jnp.bfloat16)] * len(whiches),
        in_specs=[SMEM, SMEM] + [ANY] * sum(counts) + [VMEM] * len(arrays),
        out_specs=[VMEM] * len(whiches),
        scratch_shapes=[
            pltpu.VMEM((SECTORS * lon, pieces[0].shape[1], chans), jnp.bfloat16) for pieces in sets
        ]
        + [
            pltpu.VMEM((half * RG, K * 2 * chans), jnp.bfloat16),
            pltpu.VMEM((2, half * RG, chans), jnp.float32),
            pltpu.SemaphoreType.DMA((len(sets), SECTORS)),
        ],
        compiler_params=pltpu.CompilerParams(vmem_limit_bytes=24 << 20),
        cost_estimate=pl.CostEstimate(flops=1, bytes_accessed=1, transcendentals=0),
    )(place, shifts, *[x for pieces in sets for x in pieces], *arrays)


def together(*values):
    return lax.optimization_barrier(values)


def on_device(field, filters, sector_width, block_offset, mixing):
    rows, lon, chans = field.shape
    half = chans // 2
    lat = lax.axis_index("lat")
    upper, core = lat // 2, lat % 2
    first = core == 0
    far = core == upper
    place = jnp.stack([upper, far.astype(jnp.int32), lax.axis_index("lon") % 2]).astype(jnp.int32)

    turned = field.transpose(1, 0, 2)
    low, high = turned[:, :, :half], turned[:, :, half:]
    mine, theirs = together(jnp.where(first, low, high), jnp.where(first, high, low))
    got = lat_swap(theirs, 1)
    filters, block_offset, mixing, mine = together(filters, block_offset, mixing, mine)
    shifts = BW * block_offset * sector_width[:, None]
    other_shifts = lat_swap(shifts, 1)
    other_filters = lat_swap(filters, 1)

    got, mine, filters, mixing = together(got, mine, filters, mixing)
    top, bottom = jnp.where(first, mine, got), jnp.where(first, got, mine)
    own = jnp.concatenate([top, bottom], axis=1)
    edge = lat_swap(jnp.where(upper == 0, bottom, top), 2)
    own_near, own_back = halo(own)

    both = jnp.stack([filters, other_filters])
    both = jnp.pad(both, ((0, 0),) * 4 + ((0, PADDED - both.shape[-1]),))
    far_left, near_left = left_sides(place, both)
    far_shifts = jnp.where(far, shifts, other_shifts)
    near_shifts = jnp.where(far, other_shifts, shifts)
    all_shifts = jnp.concatenate([far_shifts, near_shifts], axis=0)

    group_chans = chans // G
    side = lax.dynamic_slice_in_dim(mixing, core * half, half, axis=2)
    tiled = jnp.tile(side, (1, chans // group_chans, 2))
    row_at = lax.broadcasted_iota(jnp.int32, (chans, chans), 0) // group_chans
    col_at = lax.broadcasted_iota(jnp.int32, (chans, chans), 1) // group_chans
    mix = jnp.where((row_at == col_at)[None], tiled, jnp.zeros_like(tiled))
    mix = mix.reshape(K * chans, chans)
    far_left, near_left, mix, edge = together(far_left, near_left, mix, edge)

    edge_near, edge_back = halo(edge)
    own_far_near, own_far_back = beyond(own_near, own_back)
    edge_far_near, edge_far_back = beyond(edge_near, edge_back)

    own_set, edge_set = [own, own_near, own_back], [edge, edge_near, edge_back]
    done = conv([0, 1], place, all_shifts, [own_set, edge_set], [far_left, near_left], mix)
    own_far_near, own_far_back, done = together(own_far_near, own_far_back, done)
    own_set += [own_far_near, own_far_back]
    (far_out,) = conv([0], place, all_shifts, [own_set], [far_left], mix, done[:1])
    edge_far_near, edge_far_back, far_out = together(edge_far_near, edge_far_back, far_out)
    edge_set += [edge_far_near, edge_far_back]
    sets = [own_set, edge_set]
    (near_out,) = conv([1], place, all_shifts, sets, [near_left], mix, done[1:])

    far_out, near_out = (x.reshape(rows, lon, half) for x in (far_out, near_out))
    kept = jnp.where(far, far_out, near_out)
    other = lat_swap(jnp.where(far, near_out, far_out), 1)
    return jnp.concatenate([jnp.where(first, kept, other), jnp.where(first, other, kept)], axis=2)


def solution(mesh):
    return jax.shard_map(
        on_device,
        mesh=mesh,
        in_specs=(P("lat", "lon", None), P("lat", None, None, None), P("lat"), P("lat", None), P()),
        out_specs=P("lat", "lon", None),
        check_vma=False,
    )
```

```python
import functools

import jax
import jax.numpy as jnp
from jax import lax
from jax.experimental import pallas as pl
from jax.experimental.pallas import tpu as pltpu
from jax.sharding import PartitionSpec as P

K = 9
G = 8
R = 16
RG = 8
NB = 4
BW = 8
SMAX = 2
J = 2
T = BW + J - 1
SECTORS = 2 * SMAX + 1
PADDED = 384
VMEM = pl.BlockSpec(memory_space=pltpu.VMEM)
SMEM = pl.BlockSpec(memory_space=pltpu.SMEM)
ANY = pl.BlockSpec(memory_space=pl.ANY)


def lat_swap(value, flip):
    return lax.ppermute(value, "lat", [(lat, lat ^ flip) for lat in range(4)])


def pair_swap(value, odd):
    count = lax.axis_size("lon")
    pairs = [(s, (((s + odd) ^ 1) - odd) % count) for s in range(count)]
    return lax.ppermute(value, "lon", pairs)


def halo(value):
    near, back = pair_swap(value, 0), pair_swap(value, 1)
    return near, back


def beyond(near, back):
    return pair_swap(back, 0), pair_swap(near, 1)


def prep_kernel(place_ref, filt_ref, far_ref, near_ref, spread_ref, pick_ref):
    upper = place_ref[0]
    far = place_ref[1]
    deep, wide = NB * 128, T * NB * R

    row = lax.broadcasted_iota(jnp.int32, (deep, wide), 0)
    col = lax.broadcasted_iota(jnp.int32, (1, wide), 1)
    for j in range(J):
        t = (col >> 6) - j
        target = ((col >> 4) & 3) * 128 + (col & 15) * BW + t
        hit = jnp.where((row == target) & (t >= 0) & (t < BW), 1.0, 0.0)
        pick_ref[j] = hit.astype(jnp.bfloat16)

    for which in range(2):
        half = jnp.where(far == 1, which, 1 - which)
        base = 1 - upper if which == 0 else upper
        for g in range(2):
            for p in range(RG):
                i = g * RG + p
                for b in range(NB):
                    x = filt_ref[half, i, b].astype(jnp.float32)
                    if i:
                        x = pltpu.roll(x, BW * i, 1)
                    for n in range(PADDED // 128):
                        spread_ref[n, b, pl.ds(p, K, stride=RG), :] = x[:, n * 128 : (n + 1) * 128]

            def lay(band, n):
                left = jnp.concatenate([spread_ref[band, b] for b in range(NB)], axis=1)
                left = left.astype(jnp.bfloat16)
                sides = [
                    jnp.dot(left, pick_ref[j], preferred_element_type=jnp.float32)
                    for j in range(J)
                ]
                for k in range(K):
                    both = jnp.concatenate([s[k * RG : (k + 1) * RG] for s in sides], axis=0)
                    columns = slice(n * wide, (n + 1) * wide)
                    ref = (far_ref, near_ref)[which]
                    ref[g, k * 16 : (k + 1) * 16, columns] = both.astype(jnp.bfloat16)

            lay(base, 0)
            lay(base + 1, 1)
            if which:
                lay(2 * (1 - upper), 2)


def left_sides(place, filters):
    wide = T * NB * R
    return pl.pallas_call(
        prep_kernel,
        out_shape=[
            jax.ShapeDtypeStruct((2, K * J * RG, sets * wide), jnp.bfloat16) for sets in (2, 3)
        ],
        in_specs=[SMEM, VMEM],
        out_specs=[VMEM] * 2,
        scratch_shapes=[
            pltpu.VMEM((PADDED // 128, NB, K * RG, 128), jnp.float32),
            pltpu.VMEM((J, NB * 128, wide), jnp.bfloat16),
        ],
        compiler_params=pltpu.CompilerParams(vmem_limit_bytes=16 << 20),
        cost_estimate=pl.CostEstimate(flops=1, bytes_accessed=1, transcendentals=0),
    )(place, filters)


def fetch(place_ref, pieces, ext, sems):
    lon = pieces[0].shape[0]
    odd = place_ref[2]
    sectors = (SMAX, 3 - 2 * odd, 1 + 2 * odd, 4 - 4 * odd, 4 * odd)
    copies = []
    for n, piece in enumerate(pieces):
        target = ext.at[pl.ds(sectors[n] * lon, lon)]
        copies.append(pltpu.make_async_copy(piece, target, sems.at[n]))
    return copies


def product(left, exts, shifts, jb, lon):
    columns = []
    for side in range(2):
        at = SMAX * lon + jb * J + side * (lon // 2)
        starts = [at + shift for shift in shifts]
        rows = []
        for ext in exts:
            for first in range(0, ext.shape[1], R):
                for t in range(T):
                    for start in starts:
                        rows.append(ext[start + t, first : first + R, :])
        columns.append(jnp.concatenate(rows, axis=0))
    right = jnp.concatenate(columns, axis=1)
    return jnp.dot(left, right, preferred_element_type=jnp.float32)


def keep(resp_ref, resp, jb):
    resp = resp.astype(jnp.bfloat16)
    width = resp.shape[1]
    rows = pl.ds(pl.multiple_of(jb * 16, 16), 16)
    for k in range(K):
        resp_ref[rows, k * width : (k + 1) * width] = resp[k * 16 : (k + 1) * 16]


def mix_rows(resp_ref, mix_ref, mixed_ref, out_ref, g):
    mixed = jnp.dot(resp_ref[...], mix_ref[...], preferred_element_type=jnp.float32)
    chans = mixed.shape[1] // 2
    half = mixed.shape[0] // RG
    for side in range(2):
        mixed_ref[side] = mixed[:, side * chans : (side + 1) * chans]
        for p in range(RG):
            rows = mixed_ref[side, pl.ds(p, half, stride=RG), :]
            out_ref[g, p, side * half : (side + 1) * half, :] = rows.astype(jnp.bfloat16)


def conv_kernel(early, whiches, counts, place_ref, shift_ref, *refs):
    sets = []
    for count in counts:
        sets.append(refs[:count])
        refs = refs[count:]
    some = len(whiches)
    left_refs, mix_ref, refs = refs[:some], refs[some], refs[some + 1 :]
    if not early:
        done_refs, refs = refs[:some], refs[some:]
    out_refs, refs = refs[:some], refs[some:]
    exts, (resp_ref, mixed_ref, sems) = refs[: len(sets)], refs[len(sets) :]
    lon = sets[0][0].shape[0]
    copies = []
    for i, pieces in enumerate(sets):
        copies += fetch(place_ref, pieces, exts[i], sems.at[i])
    for copy in copies:
        copy.start()
    for copy in copies:
        copy.wait()
    for n, which in enumerate(whiches):
        left_ref, out_ref = left_refs[n], out_refs[n]

        def group(g, carry):
            shifts = [shift_ref[2 * which + g, b] for b in range(NB)]
            local = True
            for shift in shifts:
                local = local & (shift >= -lon) & (shift <= lon - BW)

            @pl.when(local if early else jnp.logical_not(local))
            def _():
                def step(jb, carry):
                    keep(resp_ref, product(left_ref[g], exts[: 1 + which], shifts, jb, lon), jb)
                    return carry

                lax.fori_loop(0, lon // 2 // J, step, 0, unroll=True)
                mix_rows(resp_ref, mix_ref, mixed_ref, out_ref, g)

            if not early:

                @pl.when(local)
                def _():
                    out_ref[g] = done_refs[n][g]

            return carry

        lax.fori_loop(0, 2, group, 0)


def conv(whiches, place, shifts, sets, lefts, mix, done=()):
    lon, _, chans = sets[0][0].shape
    half = lon // 2
    counts = [len(pieces) for pieces in sets]
    arrays = [*lefts, mix, *done]
    return pl.pallas_call(
        functools.partial(conv_kernel, not done, whiches, counts),
        out_shape=[jax.ShapeDtypeStruct((2, RG, lon, chans), jnp.bfloat16)] * len(whiches),
        in_specs=[SMEM, SMEM] + [ANY] * sum(counts) + [VMEM] * len(arrays),
        out_specs=[VMEM] * len(whiches),
        scratch_shapes=[
            pltpu.VMEM((SECTORS * lon, pieces[0].shape[1], chans), jnp.bfloat16) for pieces in sets
        ]
        + [
            pltpu.VMEM((half * RG, K * 2 * chans), jnp.bfloat16),
            pltpu.VMEM((2, half * RG, chans), jnp.float32),
            pltpu.SemaphoreType.DMA((len(sets), SECTORS)),
        ],
        compiler_params=pltpu.CompilerParams(vmem_limit_bytes=24 << 20),
        cost_estimate=pl.CostEstimate(flops=1, bytes_accessed=1, transcendentals=0),
    )(place, shifts, *[x for pieces in sets for x in pieces], *arrays)


def together(*values):
    return lax.optimization_barrier(values)


def on_device(field, filters, sector_width, block_offset, mixing):
    rows, lon, chans = field.shape
    half = chans // 2
    lat = lax.axis_index("lat")
    upper, core = lat // 2, lat % 2
    first = core == 0
    far = core == upper
    place = jnp.stack([upper, far.astype(jnp.int32), lax.axis_index("lon") % 2]).astype(jnp.int32)

    turned = field.transpose(1, 0, 2)
    low, high = turned[:, :, :half], turned[:, :, half:]
    mine, theirs = together(jnp.where(first, low, high), jnp.where(first, high, low))
    got = lat_swap(theirs, 1)
    filters, block_offset, mixing, mine = together(filters, block_offset, mixing, mine)
    shifts = BW * block_offset * sector_width[:, None]
    other_shifts = lat_swap(shifts, 1)
    other_filters = lat_swap(filters, 1)

    got, mine, filters, mixing = together(got, mine, filters, mixing)
    top, bottom = jnp.where(first, mine, got), jnp.where(first, got, mine)
    own = jnp.concatenate([top, bottom], axis=1)
    edge = lat_swap(jnp.where(upper == 0, bottom, top), 2)
    own_near = pair_swap(own, 0)
    own_late, edge, filters, other_filters, mixing = together(
        own, edge, filters, other_filters, mixing
    )
    own_back = pair_swap(own_late, 1)
    edge_near, edge_back = halo(edge)

    both = jnp.stack([filters, other_filters])
    both = jnp.pad(both, ((0, 0),) * 4 + ((0, PADDED - both.shape[-1]),))
    far_left, near_left = left_sides(place, both)
    far_shifts = jnp.where(far, shifts, other_shifts)
    near_shifts = jnp.where(far, other_shifts, shifts)
    all_shifts = jnp.concatenate([far_shifts, near_shifts], axis=0)

    group_chans = chans // G
    side = lax.dynamic_slice_in_dim(mixing, core * half, half, axis=2)
    tiled = jnp.tile(side, (1, chans // group_chans, 2))
    row_at = lax.broadcasted_iota(jnp.int32, (chans, chans), 0) // group_chans
    col_at = lax.broadcasted_iota(jnp.int32, (chans, chans), 1) // group_chans
    mix = jnp.where((row_at == col_at)[None], tiled, jnp.zeros_like(tiled))
    mix = mix.reshape(K * chans, chans)

    far_left, near_left, mix, own_near, own_back = together(
        far_left, near_left, mix, own_near, own_back
    )
    own_far_near, own_far_back = beyond(own_near, own_back)
    own_set, edge_set = [own, own_near, own_back], [edge, edge_near, edge_back]
    (far_done,) = conv([0], place, all_shifts, [own_set], [far_left], mix)
    edge_near, edge_back, far_done = together(edge_near, edge_back, far_done)
    edge_set = [edge, edge_near, edge_back]
    edge_far_near, edge_far_back = beyond(edge_near, edge_back)
    (near_done,) = conv([1], place, all_shifts, [own_set, edge_set], [near_left], mix)
    own_far_near, own_far_back, near_done = together(own_far_near, own_far_back, near_done)
    own_set = own_set + [own_far_near, own_far_back]
    (far_out,) = conv([0], place, all_shifts, [own_set], [far_left], mix, [far_done])
    edge_far_near, edge_far_back, far_out = together(edge_far_near, edge_far_back, far_out)
    edge_set = edge_set + [edge_far_near, edge_far_back]
    sets = [own_set, edge_set]
    (near_out,) = conv([1], place, all_shifts, sets, [near_left], mix, [near_done])

    far_out, near_out = (x.reshape(rows, lon, half) for x in (far_out, near_out))
    kept = jnp.where(far, far_out, near_out)
    other = lat_swap(jnp.where(far, near_out, far_out), 1)
    return jnp.concatenate([jnp.where(first, kept, other), jnp.where(first, other, kept)], axis=2)


def solution(mesh):
    return jax.shard_map(
        on_device,
        mesh=mesh,
        in_specs=(P("lat", "lon", None), P("lat", None, None, None), P("lat"), P("lat", None), P()),
        out_specs=P("lat", "lon", None),
        check_vma=False,
    )
```

```python
import functools

import jax
import jax.numpy as jnp
from jax import lax
from jax.experimental import pallas as pl
from jax.experimental.pallas import tpu as pltpu
from jax.sharding import PartitionSpec as P

K = 9
G = 8
R = 16
RG = 8
NB = 4
BW = 8
SMAX = 2
J = 2
T = BW + J - 1
SECTORS = 2 * SMAX + 1
PADDED = 384
VMEM = pl.BlockSpec(memory_space=pltpu.VMEM)
SMEM = pl.BlockSpec(memory_space=pltpu.SMEM)
ANY = pl.BlockSpec(memory_space=pl.ANY)


def lat_swap(value, flip):
    return lax.ppermute(value, "lat", [(lat, lat ^ flip) for lat in range(4)])


def pair_swap(value, odd):
    count = lax.axis_size("lon")
    pairs = [(s, (((s + odd) ^ 1) - odd) % count) for s in range(count)]
    return lax.ppermute(value, "lon", pairs)


def halo(value):
    near, back = pair_swap(value, 0), pair_swap(value, 1)
    return near, back


def prep_kernel(place_ref, filt_ref, far_ref, near_ref, spread_ref, pick_ref):
    upper = place_ref[0]
    far = place_ref[1]
    deep, wide = NB * 128, T * NB * R

    row = lax.broadcasted_iota(jnp.int32, (deep, wide), 0)
    col = lax.broadcasted_iota(jnp.int32, (1, wide), 1)
    for j in range(J):
        t = (col >> 6) - j
        target = ((col >> 4) & 3) * 128 + (col & 15) * BW + t
        hit = jnp.where((row == target) & (t >= 0) & (t < BW), 1.0, 0.0)
        pick_ref[j] = hit.astype(jnp.bfloat16)

    for which in range(2):
        half = jnp.where(far == 1, which, 1 - which)
        base = 1 - upper if which == 0 else upper
        for g in range(2):
            for p in range(RG):
                i = g * RG + p
                for b in range(NB):
                    x = filt_ref[half, i, b].astype(jnp.float32)
                    if i:
                        x = pltpu.roll(x, BW * i, 1)
                    for n in range(PADDED // 128):
                        spread_ref[n, b, pl.ds(p, K, stride=RG), :] = x[:, n * 128 : (n + 1) * 128]

            def lay(band, n):
                left = jnp.concatenate([spread_ref[band, b] for b in range(NB)], axis=1)
                left = left.astype(jnp.bfloat16)
                sides = [
                    jnp.dot(left, pick_ref[j], preferred_element_type=jnp.float32)
                    for j in range(J)
                ]
                for k in range(K):
                    both = jnp.concatenate([s[k * RG : (k + 1) * RG] for s in sides], axis=0)
                    columns = slice(n * wide, (n + 1) * wide)
                    ref = (far_ref, near_ref)[which]
                    ref[g, k * 16 : (k + 1) * 16, columns] = both.astype(jnp.bfloat16)

            lay(base, 0)
            lay(base + 1, 1)
            if which:
                lay(2 * (1 - upper), 2)


def left_sides(place, filters):
    wide = T * NB * R
    return pl.pallas_call(
        prep_kernel,
        out_shape=[
            jax.ShapeDtypeStruct((2, K * J * RG, sets * wide), jnp.bfloat16) for sets in (2, 3)
        ],
        in_specs=[SMEM, VMEM],
        out_specs=[VMEM] * 2,
        scratch_shapes=[
            pltpu.VMEM((PADDED // 128, NB, K * RG, 128), jnp.float32),
            pltpu.VMEM((J, NB * 128, wide), jnp.bfloat16),
        ],
        compiler_params=pltpu.CompilerParams(vmem_limit_bytes=16 << 20),
        cost_estimate=pl.CostEstimate(flops=1, bytes_accessed=1, transcendentals=0),
    )(place, filters)


def fetch(place_ref, pieces, ext, sems):
    lon = pieces[0].shape[0]
    odd = place_ref[2]
    sectors = (SMAX, 3 - 2 * odd, 1 + 2 * odd, 4 - 4 * odd, 4 * odd)
    copies = []
    for n, piece in enumerate(pieces):
        target = ext.at[pl.ds(sectors[n] * lon, lon)]
        copies.append(pltpu.make_async_copy(piece, target, sems.at[n]))
    return copies


def product(left, exts, shifts, jb, lon):
    columns = []
    for side in range(2):
        at = SMAX * lon + jb * J + side * (lon // 2)
        starts = [at + shift for shift in shifts]
        rows = []
        for ext in exts:
            for first in range(0, ext.shape[1], R):
                for t in range(T):
                    for start in starts:
                        rows.append(ext[start + t, first : first + R, :])
        columns.append(jnp.concatenate(rows, axis=0))
    right = jnp.concatenate(columns, axis=1)
    return jnp.dot(left, right, preferred_element_type=jnp.float32)


def keep(resp_ref, resp, jb):
    resp = resp.astype(jnp.bfloat16)
    width = resp.shape[1]
    rows = pl.ds(pl.multiple_of(jb * 16, 16), 16)
    for k in range(K):
        resp_ref[rows, k * width : (k + 1) * width] = resp[k * 16 : (k + 1) * 16]


def mix_rows(resp_ref, mix_ref, mixed_ref, out_ref, g):
    mixed = jnp.dot(resp_ref[...], mix_ref[...], preferred_element_type=jnp.float32)
    chans = mixed.shape[1] // 2
    half = mixed.shape[0] // RG
    for side in range(2):
        mixed_ref[side] = mixed[:, side * chans : (side + 1) * chans]
        for p in range(RG):
            rows = mixed_ref[side, pl.ds(p, half, stride=RG), :]
            out_ref[g, p, side * half : (side + 1) * half, :] = rows.astype(jnp.bfloat16)


def conv_kernel(early, whiches, counts, place_ref, shift_ref, *refs):
    sets = []
    for count in counts:
        sets.append(refs[:count])
        refs = refs[count:]
    some = len(whiches)
    left_refs, mix_ref, refs = refs[:some], refs[some], refs[some + 1 :]
    if not early:
        done_refs, refs = refs[:some], refs[some:]
    out_refs, refs = refs[:some], refs[some:]
    exts, (resp_ref, mixed_ref, sems) = refs[: len(sets)], refs[len(sets) :]
    lon = sets[0][0].shape[0]

    def is_local(group):
        local = True
        for b in range(NB):
            shift = shift_ref[group, b]
            local = local & (shift >= -lon) & (shift <= lon - BW)
        return local

    flags = [is_local(2 * which + g) for which in whiches for g in range(2)]
    flags = flags if early else [jnp.logical_not(flag) for flag in flags]

    @pl.when(functools.reduce(jnp.logical_or, flags))
    def _():
        copies = []
        for i, pieces in enumerate(sets):
            copies += fetch(place_ref, pieces, exts[i], sems.at[i])
        for copy in copies:
            copy.start()
        for copy in copies:
            copy.wait()

    for n, which in enumerate(whiches):
        left_ref, out_ref = left_refs[n], out_refs[n]

        def group(g, carry):
            shifts = [shift_ref[2 * which + g, b] for b in range(NB)]
            local = is_local(2 * which + g)

            @pl.when(local if early else jnp.logical_not(local))
            def _():
                def step(jb, carry):
                    keep(resp_ref, product(left_ref[g], exts[: 1 + which], shifts, jb, lon), jb)
                    return carry

                lax.fori_loop(0, lon // 2 // J, step, 0, unroll=True)
                mix_rows(resp_ref, mix_ref, mixed_ref, out_ref, g)

            if not early:

                @pl.when(local)
                def _():
                    out_ref[g] = done_refs[n][g]

            return carry

        lax.fori_loop(0, 2, group, 0)


def conv(whiches, place, shifts, sets, lefts, mix, done=()):
    lon, _, chans = sets[0][0].shape
    half = lon // 2
    counts = [len(pieces) for pieces in sets]
    arrays = [*lefts, mix, *done]
    return pl.pallas_call(
        functools.partial(conv_kernel, not done, whiches, counts),
        out_shape=[jax.ShapeDtypeStruct((2, RG, lon, chans), jnp.bfloat16)] * len(whiches),
        in_specs=[SMEM, SMEM] + [ANY] * sum(counts) + [VMEM] * len(arrays),
        out_specs=[VMEM] * len(whiches),
        scratch_shapes=[
            pltpu.VMEM((SECTORS * lon, pieces[0].shape[1], chans), jnp.bfloat16) for pieces in sets
        ]
        + [
            pltpu.VMEM((half * RG, K * 2 * chans), jnp.bfloat16),
            pltpu.VMEM((2, half * RG, chans), jnp.float32),
            pltpu.SemaphoreType.DMA((len(sets), SECTORS)),
        ],
        compiler_params=pltpu.CompilerParams(vmem_limit_bytes=24 << 20),
        cost_estimate=pl.CostEstimate(flops=1, bytes_accessed=1, transcendentals=0),
    )(place, shifts, *[x for pieces in sets for x in pieces], *arrays)


def together(*values):
    return lax.optimization_barrier(values)


def on_device(field, filters, sector_width, block_offset, mixing):
    rows, lon, chans = field.shape
    half = chans // 2
    lat = lax.axis_index("lat")
    upper, core = lat // 2, lat % 2
    first = core == 0
    far = core == upper
    place = jnp.stack([upper, far.astype(jnp.int32), lax.axis_index("lon") % 2]).astype(jnp.int32)

    turned = field.transpose(1, 0, 2)
    low, high = turned[:, :, :half], turned[:, :, half:]
    mine, theirs = together(jnp.where(first, low, high), jnp.where(first, high, low))
    got = lat_swap(theirs, 1)
    filters, block_offset, mixing, mine = together(filters, block_offset, mixing, mine)
    shifts = BW * block_offset * sector_width[:, None]
    other_shifts = lat_swap(shifts, 1)
    other_filters = lat_swap(filters, 1)

    got, mine, filters, mixing = together(got, mine, filters, mixing)
    top, bottom = jnp.where(first, mine, got), jnp.where(first, got, mine)
    own = jnp.concatenate([top, bottom], axis=1)
    edge = lat_swap(jnp.where(upper == 0, bottom, top), 2)
    own_near = pair_swap(own, 0)
    own_late, edge, filters, other_filters, mixing = together(
        own, edge, filters, other_filters, mixing
    )
    own_back = pair_swap(own_late, 1)
    edge_near, edge_back = halo(edge)

    both = jnp.stack([filters, other_filters])
    both = jnp.pad(both, ((0, 0),) * 4 + ((0, PADDED - both.shape[-1]),))
    far_left, near_left = left_sides(place, both)
    far_shifts = jnp.where(far, shifts, other_shifts)
    near_shifts = jnp.where(far, other_shifts, shifts)
    all_shifts = jnp.concatenate([far_shifts, near_shifts], axis=0)

    group_chans = chans // G
    side = lax.dynamic_slice_in_dim(mixing, core * half, half, axis=2)
    tiled = jnp.tile(side, (1, chans // group_chans, 2))
    row_at = lax.broadcasted_iota(jnp.int32, (chans, chans), 0) // group_chans
    col_at = lax.broadcasted_iota(jnp.int32, (chans, chans), 1) // group_chans
    mix = jnp.where((row_at == col_at)[None], tiled, jnp.zeros_like(tiled))
    mix = mix.reshape(K * chans, chans)

    own_near, far_left, near_left, mix = together(own_near, far_left, near_left, mix)
    own_far_back = pair_swap(own_near, 1)
    own_far_near = pair_swap(own_back, 0)
    own_set, edge_set = [own, own_near, own_back], [edge, edge_near, edge_back]
    (far_done,) = conv([0], place, all_shifts, [own_set], [far_left], mix)
    edge_far_back = pair_swap(edge_near, 1)
    edge_back, far_done = together(edge_back, far_done)
    edge_far_near = pair_swap(edge_back, 0)
    edge_set = [edge, edge_near, edge_back]
    (near_done,) = conv([1], place, all_shifts, [own_set, edge_set], [near_left], mix)
    own_far_near, own_far_back, near_done = together(own_far_near, own_far_back, near_done)
    own_set = own_set + [own_far_near, own_far_back]
    (far_out,) = conv([0], place, all_shifts, [own_set], [far_left], mix, [far_done])
    edge_far_near, edge_far_back, far_out = together(edge_far_near, edge_far_back, far_out)
    edge_set = edge_set + [edge_far_near, edge_far_back]
    sets = [own_set, edge_set]
    (near_out,) = conv([1], place, all_shifts, sets, [near_left], mix, [near_done])

    far_out, near_out = (x.reshape(rows, lon, half) for x in (far_out, near_out))
    kept = jnp.where(far, far_out, near_out)
    other = lat_swap(jnp.where(far, near_out, far_out), 1)
    return jnp.concatenate([jnp.where(first, kept, other), jnp.where(first, other, kept)], axis=2)


def solution(mesh):
    return jax.shard_map(
        on_device,
        mesh=mesh,
        in_specs=(P("lat", "lon", None), P("lat", None, None, None), P("lat"), P("lat", None), P()),
        out_specs=P("lat", "lon", None),
        check_vma=False,
    )
```

```python
import functools

import jax
import jax.numpy as jnp
from jax import lax
from jax.experimental import pallas as pl
from jax.experimental.pallas import tpu as pltpu
from jax.sharding import PartitionSpec as P

K = 9
G = 8
R = 16
RG = 8
NB = 4
BW = 8
SMAX = 2
J = 2
T = BW + J - 1
SECTORS = 2 * SMAX + 1
PADDED = 384
VMEM = pl.BlockSpec(memory_space=pltpu.VMEM)
SMEM = pl.BlockSpec(memory_space=pltpu.SMEM)
ANY = pl.BlockSpec(memory_space=pl.ANY)


def lat_swap(value, flip):
    return lax.ppermute(value, "lat", [(lat, lat ^ flip) for lat in range(4)])


def pair_swap(value, odd):
    count = lax.axis_size("lon")
    pairs = [(s, (((s + odd) ^ 1) - odd) % count) for s in range(count)]
    return lax.ppermute(value, "lon", pairs)


def halo(value):
    near, back = pair_swap(value, 0), pair_swap(value, 1)
    return near, back


def prep_kernel(place_ref, filt_ref, far_ref, near_ref, spread_ref, pick_ref):
    upper = place_ref[0]
    far = place_ref[1]
    deep, wide = NB * 128, T * NB * R

    row = lax.broadcasted_iota(jnp.int32, (deep, wide), 0)
    col = lax.broadcasted_iota(jnp.int32, (1, wide), 1)
    for j in range(J):
        t = (col >> 6) - j
        target = ((col >> 4) & 3) * 128 + (col & 15) * BW + t
        hit = jnp.where((row == target) & (t >= 0) & (t < BW), 1.0, 0.0)
        pick_ref[j] = hit.astype(jnp.bfloat16)

    for which in range(2):
        half = jnp.where(far == 1, which, 1 - which)
        base = 1 - upper if which == 0 else upper
        for g in range(2):
            for p in range(RG):
                i = g * RG + p
                for b in range(NB):
                    x = filt_ref[half, i, b].astype(jnp.float32)
                    if i:
                        x = pltpu.roll(x, BW * i, 1)
                    for n in range(PADDED // 128):
                        spread_ref[n, b, pl.ds(p, K, stride=RG), :] = x[:, n * 128 : (n + 1) * 128]

            def lay(band, n):
                left = jnp.concatenate([spread_ref[band, b] for b in range(NB)], axis=1)
                left = left.astype(jnp.bfloat16)
                sides = [
                    jnp.dot(left, pick_ref[j], preferred_element_type=jnp.float32)
                    for j in range(J)
                ]
                for k in range(K):
                    both = jnp.concatenate([s[k * RG : (k + 1) * RG] for s in sides], axis=0)
                    columns = slice(n * wide, (n + 1) * wide)
                    ref = (far_ref, near_ref)[which]
                    ref[g, k * 16 : (k + 1) * 16, columns] = both.astype(jnp.bfloat16)

            lay(base, 0)
            lay(base + 1, 1)
            if which:
                lay(2 * (1 - upper), 2)


def left_sides(place, filters):
    wide = T * NB * R
    return pl.pallas_call(
        prep_kernel,
        out_shape=[
            jax.ShapeDtypeStruct((2, K * J * RG, sets * wide), jnp.bfloat16) for sets in (2, 3)
        ],
        in_specs=[SMEM, VMEM],
        out_specs=[VMEM] * 2,
        scratch_shapes=[
            pltpu.VMEM((PADDED // 128, NB, K * RG, 128), jnp.float32),
            pltpu.VMEM((J, NB * 128, wide), jnp.bfloat16),
        ],
        compiler_params=pltpu.CompilerParams(vmem_limit_bytes=16 << 20),
        cost_estimate=pl.CostEstimate(flops=1, bytes_accessed=1, transcendentals=0),
    )(place, filters)


def fetch(place_ref, pieces, ext, sems):
    lon = pieces[0].shape[0]
    odd = place_ref[2]
    sectors = (SMAX, 3 - 2 * odd, 1 + 2 * odd, 4 - 4 * odd, 4 * odd)
    copies = []
    for n, piece in enumerate(pieces):
        target = ext.at[pl.ds(sectors[n] * lon, lon)]
        copies.append(pltpu.make_async_copy(piece, target, sems.at[n]))
    return copies


def product(left, exts, shifts, jb, lon):
    columns = []
    for side in range(2):
        at = SMAX * lon + jb * J + side * (lon // 2)
        starts = [at + shift for shift in shifts]
        rows = []
        for ext in exts:
            for first in range(0, ext.shape[1], R):
                for t in range(T):
                    for start in starts:
                        rows.append(ext[start + t, first : first + R, :])
        columns.append(jnp.concatenate(rows, axis=0))
    right = jnp.concatenate(columns, axis=1)
    return jnp.dot(left, right, preferred_element_type=jnp.float32)


def keep(resp_ref, resp, jb):
    resp = resp.astype(jnp.bfloat16)
    width = resp.shape[1]
    rows = pl.ds(pl.multiple_of(jb * 16, 16), 16)
    for k in range(K):
        resp_ref[rows, k * width : (k + 1) * width] = resp[k * 16 : (k + 1) * 16]


def mix_rows(resp_ref, mix_ref, mixed_ref, out_ref, g):
    mixed = jnp.dot(resp_ref[...], mix_ref[...], preferred_element_type=jnp.float32)
    chans = mixed.shape[1] // 2
    half = mixed.shape[0] // RG
    for side in range(2):
        mixed_ref[side] = mixed[:, side * chans : (side + 1) * chans]
        for p in range(RG):
            rows = mixed_ref[side, pl.ds(p, half, stride=RG), :]
            out_ref[g, p, side * half : (side + 1) * half, :] = rows.astype(jnp.bfloat16)


def is_local(shift_ref, group, lon):
    local = True
    for b in range(NB):
        shift = shift_ref[group, b]
        local = local & (shift >= -lon) & (shift <= lon - BW)
    return local


def fetch_if(flag, place_ref, sets, exts, sems):
    @pl.when(flag)
    def _():
        copies = []
        for i, pieces in enumerate(sets):
            copies += fetch(place_ref, pieces, exts[i], sems.at[i])
        for copy in copies:
            copy.start()
        for copy in copies:
            copy.wait()


def each_group(which, shift_ref, lon, wanted, work, otherwise=None):
    body, after = work

    def group(g, carry):
        shifts = [shift_ref[2 * which + g, b] for b in range(NB)]
        local = is_local(shift_ref, 2 * which + g, lon)

        @pl.when(local if wanted else jnp.logical_not(local))
        def _():
            def step(jb, carry):
                body(g, jb, shifts)
                return carry

            lax.fori_loop(0, lon // 2 // J, step, 0, unroll=True)
            after(g)

        if otherwise is not None:

            @pl.when(jnp.logical_not(local) if wanted else local)
            def _():
                otherwise(g)

        return carry

    lax.fori_loop(0, 2, group, 0)


def conv_kernel(role, counts, place_ref, shift_ref, *refs):
    sets = []
    for count in counts:
        sets.append(refs[:count])
        refs = refs[count:]
    lon = sets[0][0].shape[0]
    width = T * NB * 2 * R
    which = role % 2
    if role < 2:
        left_ref, mix_ref, out_ref, refs = *refs[:3], refs[3:]
    elif role == 2:
        left_ref, near_ref, mix_ref, done_ref, out_ref, sums_ref, refs = *refs[:6], refs[6:]
    else:
        left_ref, mix_ref, done_ref, sums_ref, out_ref, refs = *refs[:5], refs[5:]
    exts, (resp_ref, mixed_ref, sems) = refs[: len(sets)], refs[len(sets) :]

    groups = range(4) if role == 2 else range(2 * which, 2 * which + 2)
    flags = [is_local(shift_ref, group, lon) for group in groups]
    flags = flags if role < 2 else [jnp.logical_not(flag) for flag in flags]
    fetch_if(functools.reduce(jnp.logical_or, flags), place_ref, sets, exts, sems)

    def after(g):
        mix_rows(resp_ref, mix_ref, mixed_ref, out_ref, g)

    def copy(g):
        out_ref[g] = done_ref[g]

    def body(g, jb, shifts):
        left = left_ref[g, :, width:] if role == 3 else left_ref[g]
        resp = product(left, exts, shifts, jb, lon)
        keep(resp_ref, sums_ref[g, jb] + resp if role == 3 else resp, jb)

    def add(g, jb, shifts):
        sums_ref[g, jb] = product(near_ref[g, :, :width], exts, shifts, jb, lon)

    each_group(which, shift_ref, lon, role < 2, (body, after), None if role < 2 else copy)
    if role == 2:
        each_group(1, shift_ref, lon, False, (add, lambda g: None))


def conv(role, place, shifts, sets, *arrays):
    lon, _, chans = sets[0][0].shape
    half = lon // 2
    counts = [len(pieces) for pieces in sets]
    out = [jax.ShapeDtypeStruct((2, RG, lon, chans), jnp.bfloat16)]
    if role == 2:
        out += [jax.ShapeDtypeStruct((2, half // J, K * J * RG, 2 * chans), jnp.float32)]
    return pl.pallas_call(
        functools.partial(conv_kernel, role, counts),
        out_shape=out,
        in_specs=[SMEM, SMEM] + [ANY] * sum(counts) + [VMEM] * len(arrays),
        out_specs=[VMEM] * len(out),
        scratch_shapes=[
            pltpu.VMEM((SECTORS * lon, pieces[0].shape[1], chans), jnp.bfloat16) for pieces in sets
        ]
        + [
            pltpu.VMEM((half * RG, K * 2 * chans), jnp.bfloat16),
            pltpu.VMEM((2, half * RG, chans), jnp.float32),
            pltpu.SemaphoreType.DMA((len(sets), SECTORS)),
        ],
        compiler_params=pltpu.CompilerParams(vmem_limit_bytes=24 << 20),
        cost_estimate=pl.CostEstimate(flops=1, bytes_accessed=1, transcendentals=0),
    )(place, shifts, *[x for pieces in sets for x in pieces], *arrays)


def together(*values):
    return lax.optimization_barrier(values)


def on_device(field, filters, sector_width, block_offset, mixing):
    rows, lon, chans = field.shape
    half = chans // 2
    lat = lax.axis_index("lat")
    upper, core = lat // 2, lat % 2
    first = core == 0
    far = core == upper
    place = jnp.stack([upper, far.astype(jnp.int32), lax.axis_index("lon") % 2]).astype(jnp.int32)

    turned = field.transpose(1, 0, 2)
    low, high = turned[:, :, :half], turned[:, :, half:]
    mine, theirs = together(jnp.where(first, low, high), jnp.where(first, high, low))
    got = lat_swap(theirs, 1)
    filters, block_offset, mixing, mine = together(filters, block_offset, mixing, mine)
    shifts = BW * block_offset * sector_width[:, None]
    other_shifts = lat_swap(shifts, 1)
    other_filters = lat_swap(filters, 1)

    got, mine, filters, mixing = together(got, mine, filters, mixing)
    top, bottom = jnp.where(first, mine, got), jnp.where(first, got, mine)
    own = jnp.concatenate([top, bottom], axis=1)
    edge = lat_swap(jnp.where(upper == 0, bottom, top), 2)
    own_near = pair_swap(own, 0)
    own_late, edge, filters, other_filters, mixing = together(
        own, edge, filters, other_filters, mixing
    )
    own_back = pair_swap(own_late, 1)
    edge_near, edge_back = halo(edge)

    both = jnp.stack([filters, other_filters])
    both = jnp.pad(both, ((0, 0),) * 4 + ((0, PADDED - both.shape[-1]),))
    far_left, near_left = left_sides(place, both)
    far_shifts = jnp.where(far, shifts, other_shifts)
    near_shifts = jnp.where(far, other_shifts, shifts)
    all_shifts = jnp.concatenate([far_shifts, near_shifts], axis=0)

    group_chans = chans // G
    side = lax.dynamic_slice_in_dim(mixing, core * half, half, axis=2)
    tiled = jnp.tile(side, (1, chans // group_chans, 2))
    row_at = lax.broadcasted_iota(jnp.int32, (chans, chans), 0) // group_chans
    col_at = lax.broadcasted_iota(jnp.int32, (chans, chans), 1) // group_chans
    mix = jnp.where((row_at == col_at)[None], tiled, jnp.zeros_like(tiled))
    mix = mix.reshape(K * chans, chans)

    own_near, far_left, near_left, mix = together(own_near, far_left, near_left, mix)
    own_far_back = pair_swap(own_near, 1)
    own_far_near = pair_swap(own_back, 0)
    own_set, edge_set = [own, own_near, own_back], [edge, edge_near, edge_back]
    (far_done,) = conv(0, place, all_shifts, [own_set], far_left, mix)
    edge_far_back = pair_swap(edge_near, 1)
    edge_back, far_done = together(edge_back, far_done)
    edge_far_near = pair_swap(edge_back, 0)
    edge_set = [edge, edge_near, edge_back]
    (near_done,) = conv(1, place, all_shifts, [own_set, edge_set], near_left, mix)
    own_far_near, own_far_back, near_done = together(own_far_near, own_far_back, near_done)
    own_set = own_set + [own_far_near, own_far_back]
    far_out, sums = conv(2, place, all_shifts, [own_set], far_left, near_left, mix, far_done)
    edge_far_near, edge_far_back, far_out = together(edge_far_near, edge_far_back, far_out)
    edge_set = edge_set + [edge_far_near, edge_far_back]
    (near_out,) = conv(3, place, all_shifts, [edge_set], near_left, mix, near_done, sums)

    far_out, near_out = (x.reshape(rows, lon, half) for x in (far_out, near_out))
    kept = jnp.where(far, far_out, near_out)
    other = lat_swap(jnp.where(far, near_out, far_out), 1)
    return jnp.concatenate([jnp.where(first, kept, other), jnp.where(first, other, kept)], axis=2)


def solution(mesh):
    return jax.shard_map(
        on_device,
        mesh=mesh,
        in_specs=(P("lat", "lon", None), P("lat", None, None, None), P("lat"), P("lat", None), P()),
        out_specs=P("lat", "lon", None),
        check_vma=False,
    )
```
